32 devices in a mesh: pb: 8 (over z, x), lat: 4 (over y, core).
Axes of the slice: x: 2, y: 2, z: 4, core: 2. Of those that a mesh axis runs over, the one named last changes fastest.
Arguments:
- queries: bfloat16 [4096, 322], P('pb')
- tile_ids: int32 [4096], P('pb'), may hold values from 0 to 63
- tile_table: float32 [64, 322], replicated, may hold values from -6 to 6
- valid: int32 [4096], P(('pb', 'lat')), may hold values 0 or 1
- latents: bfloat16 [16384, 512], P(('pb', 'lat')), may hold values from -6 to 6
- lat_gain: float32 [512], replicated, may hold values from 0.25 to 1.75
- query_gain: float32 [322], replicated, may hold values from 0.25 to 1.75
- w_query: bfloat16 [322, 512], replicated, may hold values from -64 to 64
- w_key: bfloat16 [512, 512], replicated, may hold values from -0.25 to 0.25
- w_value: bfloat16 [512, 512], replicated, may hold values from -0.25 to 0.25
- w_out: bfloat16 [512, 322], replicated, may hold values from -0.25 to 0.25
- mlp_gain: float32 [322], replicated, may hold values from 0.25 to 1.75
- w_hidden: bfloat16 [322, 322], replicated, may hold values from -0.3125 to 0.3125
- w_back: bfloat16 [322, 322], replicated, may hold values from -0.3125 to 0.3125
- w_flow: bfloat16 [2, 322], replicated, may hold values from -0.3125 to 0.3125
Outputs:
- flow: float32 [2, 4096], P(None, ('pb', 'lat'))
The draws below stay inside these ranges and needn't reach their ends.
All inputs are finite; a program needn't handle non-finite values. No bound on the sum of `valid` on one device may be relied on, other than what follows from the above.
Results may differ from the reference program's by a relative error of at most 0.04.
Values may be sent and summed in bfloat16 or wider, within the bound.
A program may use at most 128 MiB of HBM per device.

```python
import math
import jax
import jax.numpy as jnp
from jax import lax

DQ = 322
DL = 512
HEADS = 8
DH = 64
DA = 512
NL = 16384
TILES = 64
NQ = 4096


def draw_queries(key, part):
    first = jax.random.fold_in(key, 0)
    base = jax.random.normal(first, (NQ, DQ), jnp.float32)
    return jnp.clip(base, -6.0, 6.0).astype(jnp.bfloat16)


def draw_w_query(key, part):
    first, second = jax.random.split(jax.random.fold_in(key, 7))
    base = jax.random.normal(first, (DQ, HEADS, DH), jnp.float32)
    strength = jnp.exp(jax.random.uniform(second, (HEADS,), jnp.float32, jnp.log(10.0), jnp.log(40.0)))
    factor = strength * 8.0 / jnp.sqrt(DH * 1.0) / jnp.sqrt(DQ * 1.0)
    scaled = base * factor[None, :, None]
    return jnp.clip(scaled, -64.0, 64.0).reshape(DQ, HEADS * DH).astype(jnp.bfloat16)


def set_ends(drawn, key, least, largest):
    dims = drawn.shape
    index_at = [jax.random.randint(jax.random.fold_in(key, axis), (), 0, dims[axis]) for axis in range(len(dims))]
    drawn = drawn.at[tuple(index_at)].set(least)
    longest = dims.index(max(dims))
    index_at[longest] = (index_at[longest] + 1) % dims[longest]
    return drawn.at[tuple(index_at)].set(largest)


def steps_of(own_key, extent, pieces, smallest, high):
    factor_of, own = 1.0, jax.random.fold_in(own_key, 6)
    for axis_at, parts in pieces:
        steps = jnp.exp(jax.random.uniform(jax.random.fold_in(own, axis_at), (parts,), jnp.float32, smallest / len(pieces), high / len(pieces)))
        factor_of = factor_of * jnp.repeat(steps, extent[axis_at] // parts).reshape([-1 if axis == axis_at else 1 for axis in range(len(extent))])
    return factor_of


def centred(stream_key, extent, width, limit, cuts=(), kind=jnp.bfloat16):
    values = jax.random.normal(stream_key, extent, jnp.float32) * width
    if len(cuts) > 0:
        values = steps_of(stream_key, extent, cuts, -0.22, 0.18) * values
    return jnp.clip(values, min=-limit, max=limit).astype(kind)


def setup_inputs(seed: int = 0) -> dict:
    splits = jax.random.split(jax.random.key(seed), 16)
    return {
        "queries": draw_queries(jax.random.fold_in(splits[15], 71), 0),
        "tile_ids": set_ends(jax.random.randint(splits[1], (NQ,), 0, TILES), jax.random.fold_in(splits[1], 1), 0, TILES - 1).astype(jnp.int32),
        "tile_table": centred(splits[2], (TILES, DQ), 1.0, 6.0, (), jnp.float32),
        "valid": set_ends((jax.random.randint(splits[3], (NQ,), 0, 4) < 3).astype(jnp.int32), jax.random.fold_in(splits[3], 1), 0, 1),
        "latents": centred(splits[4], (NL, DL), 1.0, 6.0, ((0, 32),)),
        "lat_gain": jnp.clip(1.0 + 0.15 * jax.random.normal(splits[5], (DL,), jnp.float32), 0.25, 1.75),
        "query_gain": jnp.clip(1.0 + 0.15 * jax.random.normal(splits[6], (DQ,), jnp.float32), 0.25, 1.75),
        "w_query": draw_w_query(jax.random.fold_in(splits[15], 71), 0),
        "w_key": centred(splits[8], (DL, DA), DL ** -0.5, 0.25),
        "w_value": centred(splits[9], (DL, DA), DL ** -0.5, 0.25),
        "w_out": centred(splits[10], (DA, DQ), DA ** -0.5, 0.25),
        "mlp_gain": jnp.clip(1.0 + 0.15 * jax.random.normal(splits[11], (DQ,), jnp.float32), 0.25, 1.75),
        "w_hidden": centred(splits[12], (DQ, DQ), DQ ** -0.5, 0.3125),
        "w_back": centred(splits[13], (DQ, DQ), DQ ** -0.5, 0.3125),
        "w_flow": centred(splits[14], (2, DQ), DQ ** -0.5, 0.3125),
    }


def layer_norm(values, gain):
    center = values - lax.optimization_barrier(jnp.mean(values, axis=-1, keepdims=True))
    spread = lax.optimization_barrier(jnp.mean(center * center, axis=-1, keepdims=True))
    return center * lax.rsqrt(spread + 1e-05) * gain

def reference(queries, tile_ids, tile_table, valid, latents, lat_gain, query_gain, w_query, w_key, w_value, w_out, mlp_gain, w_hidden, w_back, w_flow):
    onehot = (tile_ids[:, None] == jnp.arange(TILES, dtype=jnp.int32)[None, :]).astype(jnp.float32)
    shifted = queries.astype(jnp.float32) + jnp.dot(onehot, tile_table, precision=lax.Precision.HIGHEST)
    normed = layer_norm(shifted, query_gain).astype(jnp.bfloat16)
    query_proj = jnp.dot(normed, w_query, preferred_element_type=jnp.float32).astype(jnp.bfloat16)
    lat_normed = layer_norm(latents.astype(jnp.float32), lat_gain).astype(jnp.bfloat16)
    keys = jnp.dot(lat_normed, w_key, preferred_element_type=jnp.float32).astype(jnp.bfloat16)
    values = jnp.dot(lat_normed, w_value, preferred_element_type=jnp.float32).astype(jnp.bfloat16)
    key_heads = keys.astype(jnp.float32).reshape(NL, HEADS, DH)
    value_heads = values.astype(jnp.float32).reshape(NL, HEADS, DH)
    block_rows = math.gcd(NQ, 512)

    def attend(block):
        query_heads = block.astype(jnp.float32).reshape(block_rows, HEADS, DH)
        scores = jnp.einsum('qhd,khd->hqk', query_heads, key_heads) * 0.125
        top = lax.optimization_barrier(jnp.max(scores, axis=-1, keepdims=True))
        weights = jnp.exp(scores - top)
        total = lax.optimization_barrier(jnp.sum(weights, axis=-1))
        mixed = jnp.einsum('hqk,khd->qhd', weights.astype(jnp.bfloat16).astype(jnp.float32), value_heads)
        mixed = mixed / jnp.transpose(total)[:, :, None]
        return mixed.reshape(block_rows, HEADS * DH).astype(jnp.bfloat16)
    attn = lax.map(attend, query_proj.reshape(NQ // block_rows, block_rows, HEADS * DH)).reshape(NQ, HEADS * DH)
    projected = jnp.dot(attn, w_out, preferred_element_type=jnp.float32)
    normed_two = layer_norm(projected, mlp_gain)
    hidden = jax.nn.gelu(jnp.dot(normed_two.astype(jnp.bfloat16), w_hidden, preferred_element_type=jnp.float32), approximate=False).astype(jnp.bfloat16)
    updated = (normed_two + jnp.dot(hidden, w_back, preferred_element_type=jnp.float32)).astype(jnp.bfloat16)
    flow = lax.dot_general(w_flow, updated, (((1,), (1,)), ((), ())), preferred_element_type=jnp.float32)
    return flow * valid.astype(jnp.float32)[None, :]
```

```python
import functools
import math

import jax
import jax.numpy as jnp
from jax import lax
from jax.experimental import pallas as pl
from jax.experimental.pallas import tpu as pltpu
from jax.sharding import PartitionSpec as P

HEADS = 8
DH = 64
PAIR = 2 * DH
PAIRS = HEADS // 2
NEG = -1e30
BF = jnp.bfloat16
F32 = jnp.float32
VMEM = pl.BlockSpec(memory_space=pltpu.VMEM)


def layer_norm(values, gain):
    center = values - jnp.mean(values, axis=-1, keepdims=True)
    spread = jnp.mean(center * center, axis=-1, keepdims=True)
    return center * lax.rsqrt(spread + 1e-05) * gain


def prepare_kernel(part_ref, queries, ids, table, latents, lat_gain, query_gain, w_query, q_out, lat_out):
    tiles = table.shape[0]
    rows = queries.shape[0]
    lanes = lax.broadcasted_iota(jnp.int32, (rows, tiles), 1)
    onehot = (ids[...] == lanes).astype(F32)
    shifted = queries[...].astype(F32) + jnp.dot(
        onehot, table[...], precision=lax.Precision.HIGHEST, preferred_element_type=F32
    )
    normed = layer_norm(shifted, query_gain[...]).astype(BF)
    q = jnp.dot(normed, w_query[...], preferred_element_type=F32).astype(BF)
    q_out[...] = (q.astype(F32) * (DH ** -0.5)).astype(BF)
    lat_out[...] = layer_norm(latents[...].astype(F32), lat_gain[...]).astype(BF)


def attend_kernel(parts, pieces, first, last, *refs):
    refs = list(refs)
    q_refs = [refs.pop(0) for _ in range(parts)]
    lat_refs = [refs.pop(0) for _ in range(pieces)]
    w_key, w_value = refs.pop(0), refs.pop(0)
    if not first:
        acc_in, ml_in = refs.pop(0), refs.pop(0)
    if last:
        out = refs.pop(0)
    else:
        acc_out, ml_out = refs.pop(0), refs.pop(0)
    qm, keys, vals, = refs[:3]
    if last:
        acc_out, ml_out = refs[3:5]
    share = q_refs[0].shape[0]
    rows = share * parts
    count = keys.shape[1]
    low = lax.broadcasted_iota(jnp.int32, (share, PAIR), 1) < DH
    for k in range(parts):
        for p in range(PAIRS):
            both = q_refs[k][:, p * PAIR:(p + 1) * PAIR]
            zero = jnp.zeros_like(both)
            qm[2 * p, k * share:(k + 1) * share, :] = jnp.where(low, both, zero)
            qm[2 * p + 1, k * share:(k + 1) * share, :] = jnp.where(low, zero, both)
    at = 0
    for ref in lat_refs:
        n = ref.shape[0]
        piece = ref[...]
        kk = jnp.dot(piece, w_key[...], preferred_element_type=F32).astype(BF)
        vv = jnp.dot(piece, w_value[...], preferred_element_type=F32).astype(BF)
        for p in range(PAIRS):
            keys[p, at:at + n, :] = kk[:, p * PAIR:(p + 1) * PAIR]
            vals[p, at:at + n, :PAIR] = vv[:, p * PAIR:(p + 1) * PAIR]
            vals[p, at:at + n, PAIR:] = jnp.ones((n, PAIR), BF)
        at += n
    qrows = math.gcd(rows, 256)
    half = lax.broadcasted_iota(jnp.int32, (qrows, PAIR), 1) < DH

    def pair_step(p, unused):
        for c in range(rows // qrows):
            sl = slice(c * qrows, (c + 1) * qrows)
            mixed = []
            factors = []
            for h in range(2):
                s = lax.dot_general(
                    qm[2 * p + h, sl, :], keys[p], (((1,), (1,)), ((), ())),
                    preferred_element_type=F32,
                )
                top = jnp.max(s, axis=-1, keepdims=True)
                if not first:
                    old = ml_in[2 * p + h, sl, 0:1]
                    top = jnp.maximum(top, old)
                w = jnp.exp(s - top).astype(BF)
                r = jnp.dot(w, vals[p], preferred_element_type=F32)
                total = r[:, PAIR:]
                mixed.append(r[:, :PAIR])
                if not first:
                    factor = jnp.exp(old - top)
                    factors.append(factor)
                    total = total + factor * ml_in[2 * p + h, sl, DH:DH + 1]
                ml_out[2 * p + h, sl, :] = jnp.where(half, top, total)
            new = jnp.where(half, mixed[0], mixed[1])
            if not first:
                new = new + acc_in[p, sl, :] * jnp.where(half, factors[0], factors[1])
            acc_out[p, sl, :] = new
        return unused

    lax.fori_loop(0, PAIRS, pair_step, 0)
    if last:
        lane = lax.broadcasted_iota(jnp.int32, (qrows, PAIR), 1)
        for c in range(rows // qrows):
            sl = slice(c * qrows, (c + 1) * qrows)
            stats = jnp.zeros((qrows, PAIR), F32)
            for p in range(PAIRS):
                sums = []
                for h in range(2):
                    g = 2 * p + h
                    top = ml_out[g, sl, 0:1]
                    total = ml_out[g, sl, DH:DH + 1]
                    sums.append(total)
                    level = top + jnp.log(total)
                    hi = level.astype(BF).astype(F32)
                    mid = (level - hi).astype(BF).astype(F32)
                    lo = level - hi - mid
                    stats = jnp.where(lane == g, hi, stats)
                    stats = jnp.where(lane == HEADS + g, mid, stats)
                    stats = jnp.where(lane == 2 * HEADS + g, lo, stats)
                out[sl, p * PAIR:(p + 1) * PAIR] = (
                    acc_out[p, sl, :] / jnp.where(half, sums[0], sums[1])
                ).astype(BF)
            out[sl, PAIRS * PAIR:] = stats.astype(BF)


def attend(q_parts, pieces, w_key, w_value, state, last):
    first = state is None
    rows = sum(q.shape[0] for q in q_parts)
    count = sum(p.shape[0] for p in pieces)
    acc = jax.ShapeDtypeStruct((PAIRS, rows, PAIR), F32)
    ml = jax.ShapeDtypeStruct((HEADS, rows, PAIR), F32)
    packed = jax.ShapeDtypeStruct((rows, (PAIRS + 1) * PAIR), BF)
    args = [*q_parts, *pieces, w_key, w_value] + ([] if first else list(state))
    scratch = [
        pltpu.VMEM((HEADS, rows, PAIR), BF),
        pltpu.VMEM((PAIRS, count, PAIR), BF),
        pltpu.VMEM((PAIRS, count, 2 * PAIR), BF),
    ]
    if last:
        scratch += [pltpu.VMEM(acc.shape, F32), pltpu.VMEM(ml.shape, F32)]
    wide = w_key.shape[0]
    return pl.pallas_call(
        functools.partial(attend_kernel, len(q_parts), len(pieces), first, last),
        out_shape=packed if last else (acc, ml),
        in_specs=[VMEM] * len(args),
        out_specs=VMEM if last else (VMEM, VMEM),
        scratch_shapes=scratch,
        cost_estimate=pl.CostEstimate(
            flops=16 * rows * count * wide + 4 * count * wide * wide,
            bytes_accessed=count * wide * 2 + rows * wide * 8,
            transcendentals=rows * count * HEADS,
        ),
        compiler_params=pltpu.CompilerParams(vmem_limit_bytes=56 * 1024 * 1024),
    )(*args)


def finish_kernel(parts, *refs):
    part_refs = refs[:parts]
    w_out, mlp_gain, w_hidden, w_back, w_flow, valid, flow = refs[parts:]
    rows = part_refs[0].shape[0]
    wide = PAIRS * PAIR
    levels = []
    for ref in part_refs:
        st = ref[:, wide:].astype(F32)
        levels.append(
            st[:, :HEADS] + st[:, HEADS:2 * HEADS] + st[:, 2 * HEADS:3 * HEADS]
        )
    best = functools.reduce(jnp.maximum, levels)
    shares = [jnp.exp(level - best) for level in levels]
    total = functools.reduce(jnp.add, shares)
    shares = [s / total for s in shares]
    half = lax.broadcasted_iota(jnp.int32, (rows, PAIR), 1) < DH
    projected = jnp.zeros((rows, w_out.shape[1]), F32)
    for p in range(PAIRS):
        mixed = jnp.zeros((rows, PAIR), F32)
        for ref, s in zip(part_refs, shares):
            weight = jnp.where(half, s[:, 2 * p:2 * p + 1], s[:, 2 * p + 1:2 * p + 2])
            mixed = mixed + weight * ref[:, p * PAIR:(p + 1) * PAIR].astype(F32)
        projected = projected + jnp.dot(
            mixed.astype(BF), w_out[p * PAIR:(p + 1) * PAIR, :], preferred_element_type=F32
        )
    z = layer_norm(projected, mlp_gain[...])
    pre = jnp.dot(z.astype(BF), w_hidden[...], preferred_element_type=F32)
    hidden = (0.5 * pre * (1.0 + lax.erf(pre * (0.5 ** 0.5)))).astype(BF)
    u = (z + jnp.dot(hidden, w_back[...], preferred_element_type=F32)).astype(BF)
    res = lax.dot_general(
        w_flow[...], u, (((1,), (1,)), ((), ())), preferred_element_type=F32
    )
    flow[...] = res * valid[...].astype(F32)


def local(
    queries,
    tile_ids,
    tile_table,
    valid,
    latents,
    lat_gain,
    query_gain,
    w_query,
    w_key,
    w_value,
    w_out,
    mlp_gain,
    w_hidden,
    w_back,
    w_flow,
):
    pb, lat = lax.axis_size("pb"), lax.axis_size("lat")
    both = ("pb", "lat")
    outer = math.gcd(pb, lat)
    inner = pb // outer
    group = inner * lat
    devices = pb * lat
    rows, depth = queries.shape
    share = rows // lat
    own_rows, wide = latents.shape
    tiles = tile_table.shape[0]

    def swap(value, stride):
        pairs = [(i, i ^ stride) for i in range(devices)]
        return lax.ppermute(value, both, pairs)

    def turn(value, k):
        pairs = [(i, (i + k * group) % devices) for i in range(devices)]
        return lax.ppermute(value, both, pairs)

    whole = lambda *shape: pl.BlockSpec(shape, lambda i, s: (0,) * len(shape))
    q_own, lat_own = pl.pallas_call(
        prepare_kernel,
        out_shape=(
            jax.ShapeDtypeStruct((share, w_query.shape[1]), BF),
            jax.ShapeDtypeStruct((own_rows, wide), BF),
        ),
        grid_spec=pltpu.PrefetchScalarGridSpec(
            num_scalar_prefetch=1,
            grid=(1,),
            in_specs=[
                pl.BlockSpec((share, depth), lambda i, s: (s[0], 0)),
                pl.BlockSpec((share, 1), lambda i, s: (s[0], 0)),
                whole(tiles, depth),
                whole(own_rows, wide),
                whole(1, wide),
                whole(1, depth),
                whole(*w_query.shape),
            ],
            out_specs=(whole(share, w_query.shape[1]), whole(own_rows, wide)),
        ),
    )(
        lax.axis_index("lat").reshape(1),
        queries,
        tile_ids.reshape(rows, 1),
        tile_table,
        latents,
        lat_gain.reshape(1, wide),
        query_gain.reshape(1, depth),
        w_query,
    )
    q_parts = [q_own] + [turn(q_own, k) for k in range(1, outer)]

    strides = [1 << i for i in range(1, group.bit_length() - 1)]
    assert 1 << (len(strides) + 1) == group
    halves = [lat_own[:own_rows // 2], lat_own[own_rows // 2:]]
    held = [[halves[0]], [halves[1]]]
    steps = [[lat_own, swap(lat_own, 1)]]
    orders = [strides, strides[::-1]]
    for j in range(len(strides)):
        arrived = []
        for c in range(2):
            stride = orders[c][j]
            if len(held[c]) > 2:
                held[c] = [jnp.concatenate(held[c])]
            new = [swap(piece, stride) for piece in held[c]]
            held[c] = held[c] + new
            arrived += new
        steps.append(arrived + [swap(piece, 1) for piece in arrived])
    state = None
    for j, pieces in enumerate(steps):
        state = attend(q_parts, pieces, w_key, w_value, state, j == len(steps) - 1)
    packed = state
    parts = [packed[:share]] + [
        turn(packed[k * share:(k + 1) * share], -k) for k in range(1, outer)
    ]
    args = [
        *parts, w_out, mlp_gain.reshape(1, depth), w_hidden, w_back, w_flow,
        valid.reshape(1, share),
    ]
    return pl.pallas_call(
        functools.partial(finish_kernel, outer),
        out_shape=jax.ShapeDtypeStruct((w_flow.shape[0], share), F32),
        in_specs=[VMEM] * len(args),
        out_specs=VMEM,
    )(*args)


def solution(mesh):
    placed = (
        P("pb", None),
        P("pb"),
        P(),
        P(("pb", "lat")),
        P(("pb", "lat"), None),
        P(),
        P(),
        P(),
        P(),
        P(),
        P(),
        P(),
        P(),
        P(),
        P(),
    )
    return jax.shard_map(
        local, mesh=mesh, in_specs=placed, out_specs=P(None, ("pb", "lat")), check_vma=False
    )
```

```python
import functools
import math

import jax
import jax.numpy as jnp
from jax import lax
from jax.experimental import pallas as pl
from jax.experimental.pallas import tpu as pltpu
from jax.sharding import PartitionSpec as P

HEADS = 8
DH = 64
PAIR = 2 * DH
PAIRS = HEADS // 2
NEG = -1e30
BF = jnp.bfloat16
F32 = jnp.float32
MESH = pl.DeviceIdType.MESH
VMEM = pl.BlockSpec(memory_space=pltpu.VMEM)


def layer_norm(values, gain):
    center = values - jnp.mean(values, axis=-1, keepdims=True)
    spread = jnp.mean(center * center, axis=-1, keepdims=True)
    return center * lax.rsqrt(spread + 1e-05) * gain


def peers(outer, group):
    pb, lat = lax.axis_size("pb"), lax.axis_size("lat")
    me = lax.axis_index("pb") * lat + lax.axis_index("lat")
    devices = pb * lat

    def place(i):
        return (i // lat, i % lat)

    def ahead(k):
        return place((me + k * group + devices) % devices)

    def across(stride):
        return place(me + stride * (1 - 2 * ((me // stride) % 2)))

    return ahead, across


def greet(targets):
    barrier = pltpu.get_barrier_semaphore()
    for target in targets:
        pl.semaphore_signal(barrier, inc=1, device_id=target, device_id_type=MESH)
    pl.semaphore_wait(barrier, len(targets))


def prepare_kernel(
    outer, group, stride_a, stride_b, queries, ids, table, latents, lat_gain, query_gain, w_query,
    q_out, held_a, held_b, normed_a, normed_b, got_a, got_b, q_own, q_got, send_sem, recv_sem,
):
    ahead, across = peers(outer, group)
    greet([ahead(k) for k in range(1, outer)] + [across(stride_a), across(stride_b)])
    half = latents.shape[0] // 2
    copies = []
    for src, dst, stride, at in (
        (normed_a, got_a, stride_a, outer), (normed_b, got_b, stride_b, outer + 1)
    ):
        begin = (at - outer) * half
        src[...] = layer_norm(
            latents[begin:begin + half, :].astype(F32), lat_gain[...]
        ).astype(BF)
        copy = pltpu.make_async_remote_copy(
            src_ref=src, dst_ref=dst, send_sem=send_sem.at[at], recv_sem=recv_sem.at[at],
            device_id=across(stride), device_id_type=MESH,
        )
        copy.start()
        copies.append(copy)
    tiles = table.shape[0]
    share = q_own.shape[0]
    part = lax.axis_index("lat")
    lanes = lax.broadcasted_iota(jnp.int32, (tiles, share), 0)
    onehot = (ids[pl.ds(part, 1), :] == lanes).astype(F32)
    rows = queries[pl.ds(pl.multiple_of(part * share, share), share), :]
    shifted = rows.astype(F32) + lax.dot_general(
        onehot, table[...], (((0,), (0,)), ((), ())),
        precision=lax.Precision.HIGHEST, preferred_element_type=F32,
    )
    normed = layer_norm(shifted, query_gain[...]).astype(BF)
    q = jnp.dot(normed, w_query[...], preferred_element_type=F32).astype(BF)
    q = (q.astype(F32) * (DH ** -0.5)).astype(BF)
    q_own[...] = q
    for k in range(1, outer):
        copy = pltpu.make_async_remote_copy(
            src_ref=q_own, dst_ref=q_got.at[k], send_sem=send_sem.at[k], recv_sem=recv_sem.at[k],
            device_id=ahead(k), device_id_type=MESH,
        )
        copy.start()
        copies.append(copy)
    q_out[:share, :] = q
    held_a[:half, :] = normed_a[...]
    held_b[:half, :] = normed_b[...]
    for copy in copies:
        copy.wait()
    held_a[half:, :] = got_a[...]
    held_b[half:, :] = got_b[...]
    for k in range(1, outer):
        q_out[k * share:(k + 1) * share, :] = q_got[k]


def attend_kernel(pieces, first, last, *refs):
    refs = list(refs)
    q_ref = refs.pop(0)
    lat_refs = [refs.pop(0) for _ in range(pieces)]
    w_key, w_value = refs.pop(0), refs.pop(0)
    if not first:
        acc_in, stat_in = refs.pop(0), refs.pop(0)
    if last:
        out = refs.pop(0)
    else:
        acc_out, stat_out = refs.pop(0), refs.pop(0)
    keys, vals = refs
    rows = q_ref.shape[0]
    at = 0
    for ref in lat_refs:
        n = ref.shape[0]
        piece = ref[...]
        kk = jnp.dot(piece, w_key[...], preferred_element_type=F32)
        vv = jnp.dot(piece, w_value[...], preferred_element_type=F32).astype(BF)
        keys[:, at:at + n] = kk.T.astype(BF)
        for p in range(PAIRS):
            vals[p, at:at + n, :PAIR] = vv[:, p * PAIR:(p + 1) * PAIR]
            vals[p, at:at + n, PAIR:] = jnp.ones((n, PAIR), BF)
        at += n
    lane = lax.broadcasted_iota(jnp.int32, (rows, PAIR), 1)
    low = lane < DH

    def scores(g):
        p, h = g // 2, g % 2
        both = q_ref[:, p * PAIR:(p + 1) * PAIR]
        zero = jnp.zeros_like(both)
        mine = jnp.where(low, both, zero) if h == 0 else jnp.where(low, zero, both)
        return jnp.dot(mine, keys[p * PAIR:(p + 1) * PAIR, :], preferred_element_type=F32)

    stats = jnp.zeros((rows, PAIR), F32)
    ahead = scores(0)
    for g in range(HEADS):
        s = ahead
        if g + 1 < HEADS:
            ahead = scores(g + 1)
        p, h = g // 2, g % 2
        top = jnp.max(s, axis=-1, keepdims=True)
        if not first:
            old = stat_in[:, g:g + 1]
            top = jnp.maximum(top, old)
        w = jnp.exp((s - top).astype(BF))
        r = jnp.dot(w, vals[p], preferred_element_type=F32)
        total = r[:, PAIR:]
        mixed = r[:, :PAIR]
        if not first:
            factor = jnp.exp(old - top)
            total = total + factor * stat_in[:, HEADS + g:HEADS + g + 1]
            mixed = mixed + factor * acc_in[:, p * PAIR:(p + 1) * PAIR]
        if last:
            mixed = mixed / total
            level = top + jnp.log(total)
            hi = level.astype(BF).astype(F32)
            mid = (level - hi).astype(BF).astype(F32)
            stats = jnp.where(lane == g, hi, stats)
            stats = jnp.where(lane == HEADS + g, mid, stats)
            stats = jnp.where(lane == 2 * HEADS + g, level - hi - mid, stats)
        else:
            stats = jnp.where(lane == g, top, stats)
            stats = jnp.where(lane == HEADS + g, total, stats)
        if h == 0:
            kept = mixed
        else:
            new = jnp.where(low, kept, mixed)
            if last:
                out[:, p * PAIR:(p + 1) * PAIR] = new.astype(BF)
            else:
                acc_out[:, p * PAIR:(p + 1) * PAIR] = new
    if last:
        out[:, PAIRS * PAIR:] = stats.astype(BF)
    else:
        stat_out[...] = stats


def attend(q, pieces, w_key, w_value, state, last):
    first = state is None
    rows = q.shape[0]
    count = sum(p.shape[0] for p in pieces)
    acc = jax.ShapeDtypeStruct((rows, PAIRS * PAIR), F32)
    stats = jax.ShapeDtypeStruct((rows, PAIR), F32)
    packed = jax.ShapeDtypeStruct((rows, (PAIRS + 1) * PAIR), BF)
    args = [q, *pieces, w_key, w_value] + ([] if first else list(state))
    wide = w_key.shape[0]
    return pl.pallas_call(
        functools.partial(attend_kernel, len(pieces), first, last),
        out_shape=packed if last else (acc, stats),
        in_specs=[VMEM] * len(args),
        out_specs=VMEM if last else (VMEM, VMEM),
        scratch_shapes=[
            pltpu.VMEM((PAIRS * PAIR, count), BF),
            pltpu.VMEM((PAIRS, count, 2 * PAIR), BF),
        ],
        cost_estimate=pl.CostEstimate(
            flops=16 * rows * count * wide + 4 * count * wide * wide,
            bytes_accessed=count * wide * 2 + rows * wide * 8,
            transcendentals=rows * count * HEADS,
        ),
        compiler_params=pltpu.CompilerParams(vmem_limit_bytes=56 * 1024 * 1024),
    )(*args)


def finish_kernel(
    outer, group, packed, w_out, mlp_gain, w_hidden, w_back, w_flow, valid, flow,
    got, send_sem, recv_sem,
):
    ahead, across = peers(outer, group)
    greet([ahead(-k) for k in range(1, outer)])
    rows = got.shape[1]
    copies = []
    for k in range(1, outer):
        copy = pltpu.make_async_remote_copy(
            src_ref=packed.at[pl.ds(k * rows, rows)], dst_ref=got.at[k],
            send_sem=send_sem.at[k], recv_sem=recv_sem.at[k],
            device_id=ahead(-k), device_id_type=MESH,
        )
        copy.start()
        copies.append(copy)
    for copy in copies:
        copy.wait()
    part_refs = [packed.at[pl.ds(0, rows)]] + [got.at[k] for k in range(1, outer)]
    wide = PAIRS * PAIR
    levels = []
    for ref in part_refs:
        st = ref[:, wide:].astype(F32)
        levels.append(
            st[:, :HEADS] + st[:, HEADS:2 * HEADS] + st[:, 2 * HEADS:3 * HEADS]
        )
    best = functools.reduce(jnp.maximum, levels)
    shares = [jnp.exp(level - best) for level in levels]
    total = functools.reduce(jnp.add, shares)
    shares = [s / total for s in shares]
    half = lax.broadcasted_iota(jnp.int32, (rows, PAIR), 1) < DH
    projected = jnp.zeros((rows, w_out.shape[1]), F32)
    for p in range(PAIRS):
        mixed = jnp.zeros((rows, PAIR), F32)
        for ref, s in zip(part_refs, shares):
            weight = jnp.where(half, s[:, 2 * p:2 * p + 1], s[:, 2 * p + 1:2 * p + 2])
            mixed = mixed + weight * ref[:, p * PAIR:(p + 1) * PAIR].astype(F32)
        projected = projected + jnp.dot(
            mixed.astype(BF), w_out[p * PAIR:(p + 1) * PAIR, :], preferred_element_type=F32
        )
    z = layer_norm(projected, mlp_gain[...])
    pre = jnp.dot(z.astype(BF), w_hidden[...], preferred_element_type=F32)
    hidden = (0.5 * pre * (1.0 + lax.erf(pre * (0.5 ** 0.5)))).astype(BF)
    u = (z + jnp.dot(hidden, w_back[...], preferred_element_type=F32)).astype(BF)
    res = lax.dot_general(
        w_flow[...], u, (((1,), (1,)), ((), ())), preferred_element_type=F32
    )
    flow[...] = res * valid[...].astype(F32)


def local(
    queries,
    tile_ids,
    tile_table,
    valid,
    latents,
    lat_gain,
    query_gain,
    w_query,
    w_key,
    w_value,
    w_out,
    mlp_gain,
    w_hidden,
    w_back,
    w_flow,
):
    pb, lat = lax.axis_size("pb"), lax.axis_size("lat")
    both = ("pb", "lat")
    outer = math.gcd(pb, lat)
    inner = pb // outer
    group = inner * lat
    devices = pb * lat
    rows, depth = queries.shape
    share = rows // lat
    own_rows, wide = latents.shape
    tiles = tile_table.shape[0]

    def swap(value, stride):
        pairs = [(i, i ^ stride) for i in range(devices)]
        return lax.ppermute(value, both, pairs)

    strides = [1 << i for i in range(1, group.bit_length() - 1)]
    assert 1 << (len(strides) + 1) == group
    half = own_rows // 2
    da = w_query.shape[1]
    q, held_a, held_b = pl.pallas_call(
        functools.partial(prepare_kernel, outer, group, strides[0], strides[-1]),
        out_shape=(
            jax.ShapeDtypeStruct((outer * share, da), BF),
            jax.ShapeDtypeStruct((own_rows, wide), BF),
            jax.ShapeDtypeStruct((own_rows, wide), BF),
        ),
        in_specs=[VMEM] * 7,
        out_specs=(VMEM,) * 3,
        scratch_shapes=[pltpu.VMEM((half, wide), BF)] * 4 + [
            pltpu.VMEM((share, da), BF),
            pltpu.VMEM((outer, share, da), BF),
            pltpu.SemaphoreType.DMA((outer + 2,)),
            pltpu.SemaphoreType.DMA((outer + 2,)),
        ],
        compiler_params=pltpu.CompilerParams(
            collective_id=0, has_side_effects=True, vmem_limit_bytes=32 * 1024 * 1024
        ),
    )(
        queries,
        tile_ids.reshape(lat, share),
        tile_table,
        latents,
        lat_gain.reshape(1, wide),
        query_gain.reshape(1, depth),
        w_query,
    )
    held = [held_a, held_b]
    steps = [held, [swap(piece, 1) for piece in held]]
    orders = [strides, strides[::-1]]
    for j in range(1, len(strides)):
        arrived = [swap(held[c], orders[c][j]) for c in range(2)]
        steps.append(arrived + [swap(piece, 1) for piece in arrived])
        if j + 1 < len(strides):
            held = [jnp.concatenate([held[c], arrived[c]]) for c in range(2)]
    state = None
    for j, pieces in enumerate(steps):
        state = attend(q, pieces, w_key, w_value, state, j == len(steps) - 1)
    return pl.pallas_call(
        functools.partial(finish_kernel, outer, group),
        out_shape=jax.ShapeDtypeStruct((w_flow.shape[0], share), F32),
        in_specs=[VMEM] * 7,
        out_specs=VMEM,
        scratch_shapes=[
            pltpu.VMEM((outer, share, (PAIRS + 1) * PAIR), BF),
            pltpu.SemaphoreType.DMA((outer,)),
            pltpu.SemaphoreType.DMA((outer,)),
        ],
        compiler_params=pltpu.CompilerParams(
            collective_id=1, has_side_effects=True, vmem_limit_bytes=32 * 1024 * 1024
        ),
    )(
        state, w_out, mlp_gain.reshape(1, depth), w_hidden, w_back, w_flow,
        valid.reshape(1, share),
    )


def solution(mesh):
    placed = (
        P("pb", None),
        P("pb"),
        P(),
        P(("pb", "lat")),
        P(("pb", "lat"), None),
        P(),
        P(),
        P(),
        P(),
        P(),
        P(),
        P(),
        P(),
        P(),
        P(),
    )
    return jax.shard_map(
        local, mesh=mesh, in_specs=placed, out_specs=P(None, ("pb", "lat")), check_vma=False
    )
```

```python
import functools
import math

import jax
import jax.numpy as jnp
from jax import lax
from jax.experimental import pallas as pl
from jax.experimental.pallas import tpu as pltpu
from jax.sharding import PartitionSpec as P

HEADS = 8
DH = 64
PAIR = 2 * DH
PAIRS = HEADS // 2
NEG = -1e30
BF = jnp.bfloat16
F32 = jnp.float32
MESH = pl.DeviceIdType.MESH
VMEM = pl.BlockSpec(memory_space=pltpu.VMEM)


def layer_norm(values, gain):
    center = values - jnp.mean(values, axis=-1, keepdims=True)
    spread = jnp.mean(center * center, axis=-1, keepdims=True)
    return center * lax.rsqrt(spread + 1e-05) * gain


def peers(outer, group):
    pb, lat = lax.axis_size("pb"), lax.axis_size("lat")
    me = lax.axis_index("pb") * lat + lax.axis_index("lat")
    devices = pb * lat

    def place(i):
        return (i // lat, i % lat)

    def ahead(k):
        return place((me + k * group + devices) % devices)

    def across(stride):
        return place(me + stride * (1 - 2 * ((me // stride) % 2)))

    return ahead, across


def greet(targets):
    barrier = pltpu.get_barrier_semaphore()
    for target in targets:
        pl.semaphore_signal(barrier, inc=1, device_id=target, device_id_type=MESH)
    pl.semaphore_wait(barrier, len(targets))


def prepare_kernel(
    outer, group, stride_a, stride_b, queries, ids, table, latents, lat_gain, query_gain, w_query,
    q_out, held_a, held_b, normed_a, normed_b, got_a, got_b, q_own, q_got, send_sem, recv_sem,
):
    ahead, across = peers(outer, group)
    greet([ahead(k) for k in range(1, outer)] + [across(stride_a), across(stride_b)])
    copies = []
    tiles = table.shape[0]
    share = q_own.shape[0]
    part = lax.axis_index("lat")
    lanes = lax.broadcasted_iota(jnp.int32, (tiles, share), 0)
    onehot = (ids[pl.ds(part, 1), :] == lanes).astype(F32)
    rows = queries[pl.ds(pl.multiple_of(part * share, share), share), :]
    shifted = rows.astype(F32) + lax.dot_general(
        onehot, table[...], (((0,), (0,)), ((), ())),
        precision=lax.Precision.HIGHEST, preferred_element_type=F32,
    )
    normed = layer_norm(shifted, query_gain[...]).astype(BF)
    q = jnp.dot(normed, w_query[...], preferred_element_type=F32).astype(BF)
    q = (q.astype(F32) * (DH ** -0.5)).astype(BF)
    q_own[...] = q
    for k in range(1, outer):
        copy = pltpu.make_async_remote_copy(
            src_ref=q_own, dst_ref=q_got.at[k], send_sem=send_sem.at[k], recv_sem=recv_sem.at[k],
            device_id=ahead(k), device_id_type=MESH,
        )
        copy.start()
        copies.append(copy)
    half = latents.shape[0] // 2
    for src, dst, stride, at in (
        (normed_a, got_a, stride_a, outer), (normed_b, got_b, stride_b, outer + 1)
    ):
        begin = (at - outer) * half
        src[...] = layer_norm(
            latents[begin:begin + half, :].astype(F32), lat_gain[...]
        ).astype(BF)
        copy = pltpu.make_async_remote_copy(
            src_ref=src, dst_ref=dst, send_sem=send_sem.at[at], recv_sem=recv_sem.at[at],
            device_id=across(stride), device_id_type=MESH,
        )
        copy.start()
        copies.append(copy)
    q_out[:share, :] = q
    held_a[:half, :] = normed_a[...]
    held_b[:half, :] = normed_b[...]
    for copy in copies:
        copy.wait()
    held_a[half:, :] = got_a[...]
    held_b[half:, :] = got_b[...]
    for k in range(1, outer):
        q_out[k * share:(k + 1) * share, :] = q_got[k]


def attend_kernel(pieces, first, last, *refs):
    refs = list(refs)
    q_ref = refs.pop(0)
    lat_refs = [refs.pop(0) for _ in range(pieces)]
    w_key, w_value = refs.pop(0), refs.pop(0)
    if not first:
        acc_in, stat_in = refs.pop(0), refs.pop(0)
    if last:
        out = refs.pop(0)
    else:
        acc_out, stat_out = refs.pop(0), refs.pop(0)
    keys, vals = refs
    rows = q_ref.shape[0]
    at = 0
    for ref in lat_refs:
        n = ref.shape[0]
        piece = ref[...]
        kk = jnp.dot(piece, w_key[...], preferred_element_type=F32)
        vv = jnp.dot(piece, w_value[...], preferred_element_type=F32).astype(BF)
        keys[:, at:at + n] = kk.T.astype(BF)
        for p in range(PAIRS):
            vals[p, at:at + n, :PAIR] = vv[:, p * PAIR:(p + 1) * PAIR]
            vals[p, at:at + n, PAIR:] = jnp.ones((n, PAIR), BF)
        at += n
    lane = lax.broadcasted_iota(jnp.int32, (rows, PAIR), 1)
    low = lane < DH

    def scores(g):
        p, h = g // 2, g % 2
        both = q_ref[:, p * PAIR:(p + 1) * PAIR]
        zero = jnp.zeros_like(both)
        mine = jnp.where(low, both, zero) if h == 0 else jnp.where(low, zero, both)
        return jnp.dot(mine, keys[p * PAIR:(p + 1) * PAIR, :], preferred_element_type=F32)

    stats = jnp.zeros((rows, PAIR), F32)
    ahead = scores(0)
    for g in range(HEADS):
        s = ahead
        if g + 1 < HEADS:
            ahead = scores(g + 1)
        p, h = g // 2, g % 2
        top = jnp.max(s, axis=-1, keepdims=True)
        if not first:
            old = stat_in[:, g:g + 1]
            top = jnp.maximum(top, old)
        w = jnp.exp((s - top).astype(BF))
        r = jnp.dot(w, vals[p], preferred_element_type=F32)
        total = r[:, PAIR:]
        mixed = r[:, :PAIR]
        if not first:
            factor = jnp.exp(old - top)
            total = total + factor * stat_in[:, HEADS + g:HEADS + g + 1]
            mixed = mixed + factor * acc_in[:, p * PAIR:(p + 1) * PAIR]
        if last:
            mixed = mixed / total
            level = top + jnp.log(total)
            hi = level.astype(BF).astype(F32)
            mid = (level - hi).astype(BF).astype(F32)
            stats = jnp.where(lane == g, hi, stats)
            stats = jnp.where(lane == HEADS + g, mid, stats)
            stats = jnp.where(lane == 2 * HEADS + g, level - hi - mid, stats)
        else:
            stats = jnp.where(lane == g, top, stats)
            stats = jnp.where(lane == HEADS + g, total, stats)
        if h == 0:
            kept = mixed
        else:
            new = jnp.where(low, kept, mixed)
            if last:
                out[:, p * PAIR:(p + 1) * PAIR] = new.astype(BF)
            else:
                acc_out[:, p * PAIR:(p + 1) * PAIR] = new
    if last:
        out[:, PAIRS * PAIR:] = stats.astype(BF)
    else:
        stat_out[...] = stats


def attend(q, pieces, w_key, w_value, state, last):
    first = state is None
    rows = q.shape[0]
    count = sum(p.shape[0] for p in pieces)
    acc = jax.ShapeDtypeStruct((rows, PAIRS * PAIR), F32)
    stats = jax.ShapeDtypeStruct((rows, PAIR), F32)
    packed = jax.ShapeDtypeStruct((rows, (PAIRS + 1) * PAIR), BF)
    args = [q, *pieces, w_key, w_value] + ([] if first else list(state))
    wide = w_key.shape[0]
    return pl.pallas_call(
        functools.partial(attend_kernel, len(pieces), first, last),
        out_shape=packed if last else (acc, stats),
        in_specs=[VMEM] * len(args),
        out_specs=VMEM if last else (VMEM, VMEM),
        scratch_shapes=[
            pltpu.VMEM((PAIRS * PAIR, count), BF),
            pltpu.VMEM((PAIRS, count, 2 * PAIR), BF),
        ],
        cost_estimate=pl.CostEstimate(
            flops=16 * rows * count * wide + 4 * count * wide * wide,
            bytes_accessed=count * wide * 2 + rows * wide * 8,
            transcendentals=rows * count * HEADS,
        ),
        compiler_params=pltpu.CompilerParams(vmem_limit_bytes=56 * 1024 * 1024),
    )(*args)


def finish_kernel(
    outer, group, packed, w_out, mlp_gain, w_hidden, w_back, w_flow, valid, flow,
    got, send_sem, recv_sem,
):
    ahead, across = peers(outer, group)
    greet([ahead(-k) for k in range(1, outer)])
    rows = got.shape[1]
    copies = []
    for k in range(1, outer):
        copy = pltpu.make_async_remote_copy(
            src_ref=packed.at[pl.ds(k * rows, rows)], dst_ref=got.at[k],
            send_sem=send_sem.at[k], recv_sem=recv_sem.at[k],
            device_id=ahead(-k), device_id_type=MESH,
        )
        copy.start()
        copies.append(copy)
    for copy in copies:
        copy.wait()
    part_refs = [packed.at[pl.ds(0, rows)]] + [got.at[k] for k in range(1, outer)]
    wide = PAIRS * PAIR
    levels = []
    for ref in part_refs:
        st = ref[:, wide:].astype(F32)
        levels.append(
            st[:, :HEADS] + st[:, HEADS:2 * HEADS] + st[:, 2 * HEADS:3 * HEADS]
        )
    best = functools.reduce(jnp.maximum, levels)
    shares = [jnp.exp(level - best) for level in levels]
    total = functools.reduce(jnp.add, shares)
    shares = [s / total for s in shares]
    half = lax.broadcasted_iota(jnp.int32, (rows, PAIR), 1) < DH
    projected = jnp.zeros((rows, w_out.shape[1]), F32)
    for p in range(PAIRS):
        mixed = jnp.zeros((rows, PAIR), F32)
        for ref, s in zip(part_refs, shares):
            weight = jnp.where(half, s[:, 2 * p:2 * p + 1], s[:, 2 * p + 1:2 * p + 2])
            mixed = mixed + weight * ref[:, p * PAIR:(p + 1) * PAIR].astype(F32)
        projected = projected + jnp.dot(
            mixed.astype(BF), w_out[p * PAIR:(p + 1) * PAIR, :], preferred_element_type=F32
        )
    z = layer_norm(projected, mlp_gain[...])
    pre = jnp.dot(z.astype(BF), w_hidden[...], preferred_element_type=F32)
    hidden = (0.5 * pre * (1.0 + lax.erf(pre * (0.5 ** 0.5)))).astype(BF)
    u = (z + jnp.dot(hidden, w_back[...], preferred_element_type=F32)).astype(BF)
    res = lax.dot_general(
        w_flow[...], u, (((1,), (1,)), ((), ())), preferred_element_type=F32
    )
    flow[...] = res * valid[...].astype(F32)


def local(
    queries,
    tile_ids,
    tile_table,
    valid,
    latents,
    lat_gain,
    query_gain,
    w_query,
    w_key,
    w_value,
    w_out,
    mlp_gain,
    w_hidden,
    w_back,
    w_flow,
):
    pb, lat = lax.axis_size("pb"), lax.axis_size("lat")
    both = ("pb", "lat")
    outer = math.gcd(pb, lat)
    inner = pb // outer
    group = inner * lat
    devices = pb * lat
    rows, depth = queries.shape
    share = rows // lat
    own_rows, wide = latents.shape
    tiles = tile_table.shape[0]

    def swap(value, stride):
        pairs = [(i, i ^ stride) for i in range(devices)]
        return lax.ppermute(value, both, pairs)

    strides = [1 << i for i in range(1, group.bit_length() - 1)]
    assert 1 << (len(strides) + 1) == group
    half = own_rows // 2
    da = w_query.shape[1]
    q, held_a, held_b = pl.pallas_call(
        functools.partial(prepare_kernel, outer, group, strides[0], strides[-1]),
        out_shape=(
            jax.ShapeDtypeStruct((outer * share, da), BF),
            jax.ShapeDtypeStruct((own_rows, wide), BF),
            jax.ShapeDtypeStruct((own_rows, wide), BF),
        ),
        in_specs=[VMEM] * 7,
        out_specs=(VMEM,) * 3,
        scratch_shapes=[pltpu.VMEM((half, wide), BF)] * 4 + [
            pltpu.VMEM((share, da), BF),
            pltpu.VMEM((outer, share, da), BF),
            pltpu.SemaphoreType.DMA((outer + 2,)),
            pltpu.SemaphoreType.DMA((outer + 2,)),
        ],
        compiler_params=pltpu.CompilerParams(
            collective_id=0, has_side_effects=True, vmem_limit_bytes=32 * 1024 * 1024
        ),
    )(
        queries,
        tile_ids.reshape(lat, share),
        tile_table,
        latents,
        lat_gain.reshape(1, wide),
        query_gain.reshape(1, depth),
        w_query,
    )
    held = [held_a, held_b]
    orders = [strides, strides[::-1]]
    near = [swap(piece, 1) for piece in held]
    far = [swap(held[c], orders[c][1 % len(strides)]) for c in range(2)]
    state = attend(q, held, w_key, w_value, None, False)
    pending = near
    for j in range(1, len(strides)):
        far, state = lax.optimization_barrier((far, state))
        arrived = far
        near = [swap(piece, 1) for piece in arrived]
        if j + 1 < len(strides):
            held = [jnp.concatenate([held[c], arrived[c]]) for c in range(2)]
            far = [swap(held[c], orders[c][j + 1]) for c in range(2)]
        state = attend(q, pending, w_key, w_value, state, False)
        pending = arrived + near
    state = attend(q, pending, w_key, w_value, state, True)
    return pl.pallas_call(
        functools.partial(finish_kernel, outer, group),
        out_shape=jax.ShapeDtypeStruct((w_flow.shape[0], share), F32),
        in_specs=[VMEM] * 7,
        out_specs=VMEM,
        scratch_shapes=[
            pltpu.VMEM((outer, share, (PAIRS + 1) * PAIR), BF),
            pltpu.SemaphoreType.DMA((outer,)),
            pltpu.SemaphoreType.DMA((outer,)),
        ],
        compiler_params=pltpu.CompilerParams(
            collective_id=1, has_side_effects=True, vmem_limit_bytes=32 * 1024 * 1024
        ),
    )(
        state, w_out, mlp_gain.reshape(1, depth), w_hidden, w_back, w_flow,
        valid.reshape(1, share),
    )


def solution(mesh):
    placed = (
        P("pb", None),
        P("pb"),
        P(),
        P(("pb", "lat")),
        P(("pb", "lat"), None),
        P(),
        P(),
        P(),
        P(),
        P(),
        P(),
        P(),
        P(),
        P(),
        P(),
    )
    return jax.shard_map(
        local, mesh=mesh, in_specs=placed, out_specs=P(None, ("pb", "lat")), check_vma=False
    )
```

```python
import functools
import math

import jax
import jax.numpy as jnp
from jax import lax
from jax.experimental import pallas as pl
from jax.experimental.pallas import tpu as pltpu
from jax.sharding import PartitionSpec as P

HEADS = 8
DH = 64
PAIR = 2 * DH
PAIRS = HEADS // 2
NEG = -1e30
BF = jnp.bfloat16
F32 = jnp.float32
MESH = pl.DeviceIdType.MESH
VMEM = pl.BlockSpec(memory_space=pltpu.VMEM)


def layer_norm(values, gain):
    center = values - jnp.mean(values, axis=-1, keepdims=True)
    spread = jnp.mean(center * center, axis=-1, keepdims=True)
    return center * lax.rsqrt(spread + 1e-05) * gain


def peers(outer, group):
    pb, lat = lax.axis_size("pb"), lax.axis_size("lat")
    me = lax.axis_index("pb") * lat + lax.axis_index("lat")
    devices = pb * lat

    def place(i):
        return (i // lat, i % lat)

    def ahead(k):
        return place((me + k * group + devices) % devices)

    def across(stride):
        return place(me + stride * (1 - 2 * ((me // stride) % 2)))

    return ahead, across


def greet(targets):
    barrier = pltpu.get_barrier_semaphore()
    for target in targets:
        pl.semaphore_signal(barrier, inc=1, device_id=target, device_id_type=MESH)
    pl.semaphore_wait(barrier, len(targets))


def prepare_kernel(
    outer, group, stride_a, stride_b, queries, ids, table, latents, lat_gain, query_gain, w_query,
    q_out, held_a, held_b, normed_a, normed_b, got_a, got_b, q_own, q_got, send_sem, recv_sem,
):
    ahead, across = peers(outer, group)
    greet([ahead(k) for k in range(1, outer)] + [across(stride_a), across(stride_b)])
    copies = []
    tiles = table.shape[0]
    share = q_own.shape[0]
    part = lax.axis_index("lat")
    lanes = lax.broadcasted_iota(jnp.int32, (tiles, share), 0)
    onehot = (ids[pl.ds(part, 1), :] == lanes).astype(F32)
    rows = queries[pl.ds(pl.multiple_of(part * share, share), share), :]
    shifted = rows.astype(F32) + lax.dot_general(
        onehot, table[...], (((0,), (0,)), ((), ())),
        precision=lax.Precision.HIGHEST, preferred_element_type=F32,
    )
    normed = layer_norm(shifted, query_gain[...]).astype(BF)
    q = jnp.dot(normed, w_query[...], preferred_element_type=F32).astype(BF)
    q = (q.astype(F32) * (DH ** -0.5)).astype(BF)
    q_own[...] = q
    for k in range(1, outer):
        copy = pltpu.make_async_remote_copy(
            src_ref=q_own, dst_ref=q_got.at[k], send_sem=send_sem.at[k], recv_sem=recv_sem.at[k],
            device_id=ahead(k), device_id_type=MESH,
        )
        copy.start()
        copies.append(copy)
    half = latents.shape[0] // 2
    for src, dst, stride, at in (
        (normed_a, got_a, stride_a, outer), (normed_b, got_b, stride_b, outer + 1)
    ):
        begin = (at - outer) * half
        src[...] = layer_norm(
            latents[begin:begin + half, :].astype(F32), lat_gain[...]
        ).astype(BF)
        copy = pltpu.make_async_remote_copy(
            src_ref=src, dst_ref=dst, send_sem=send_sem.at[at], recv_sem=recv_sem.at[at],
            device_id=across(stride), device_id_type=MESH,
        )
        copy.start()
        copies.append(copy)
    q_out[:share, :] = q
    held_a[:half, :] = normed_a[...]
    held_b[:half, :] = normed_b[...]
    for copy in copies:
        copy.wait()
    held_a[half:, :] = got_a[...]
    held_b[half:, :] = got_b[...]
    for k in range(1, outer):
        q_out[k * share:(k + 1) * share, :] = q_got[k]


def attend_kernel(pieces, first, last, *refs, tail=None):
    refs = list(refs)
    q_ref = refs.pop(0)
    lat_refs = [refs.pop(0) for _ in range(pieces)]
    w_key, w_value = refs.pop(0), refs.pop(0)
    if not first:
        acc_in, stat_in = refs.pop(0), refs.pop(0)
    if last:
        out = refs.pop(0)
    else:
        acc_out, stat_out = refs.pop(0), refs.pop(0)
    keys, vals = refs
    rows = q_ref.shape[0]
    at = 0
    for ref in lat_refs:
        n = ref.shape[0]
        piece = ref[...]
        kk = jnp.dot(piece, w_key[...], preferred_element_type=F32)
        vv = jnp.dot(piece, w_value[...], preferred_element_type=F32).astype(BF)
        keys[:, at:at + n] = kk.T.astype(BF)
        for p in range(PAIRS):
            vals[p, at:at + n, :PAIR] = vv[:, p * PAIR:(p + 1) * PAIR]
            vals[p, at:at + n, PAIR:] = jnp.ones((n, PAIR), BF)
        at += n
    lane = lax.broadcasted_iota(jnp.int32, (rows, PAIR), 1)
    low = lane < DH

    def scores(g):
        p, h = g // 2, g % 2
        both = q_ref[:, p * PAIR:(p + 1) * PAIR]
        zero = jnp.zeros_like(both)
        mine = jnp.where(low, both, zero) if h == 0 else jnp.where(low, zero, both)
        return jnp.dot(mine, keys[p * PAIR:(p + 1) * PAIR, :], preferred_element_type=F32)

    stats = jnp.zeros((rows, PAIR), F32)
    ahead = scores(0)
    for g in range(HEADS):
        s = ahead
        if g + 1 < HEADS:
            ahead = scores(g + 1)
        p, h = g // 2, g % 2
        top = jnp.max(s, axis=-1, keepdims=True)
        if not first:
            old = stat_in[:, g:g + 1]
            top = jnp.maximum(top, old)
        w = jnp.exp((s - top).astype(BF))
        r = jnp.dot(w, vals[p], preferred_element_type=F32)
        total = r[:, PAIR:]
        mixed = r[:, :PAIR]
        if not first:
            factor = jnp.exp(old - top)
            total = total + factor * stat_in[:, HEADS + g:HEADS + g + 1]
            mixed = mixed + factor * acc_in[:, p * PAIR:(p + 1) * PAIR]
        if last:
            mixed = mixed / total
            level = top + jnp.log(total)
            hi = level.astype(BF).astype(F32)
            mid = (level - hi).astype(BF).astype(F32)
            stats = jnp.where(lane == g, hi, stats)
            stats = jnp.where(lane == HEADS + g, mid, stats)
            stats = jnp.where(lane == 2 * HEADS + g, level - hi - mid, stats)
        else:
            stats = jnp.where(lane == g, top, stats)
            stats = jnp.where(lane == HEADS + g, total, stats)
        if h == 0:
            kept = mixed
        else:
            new = jnp.where(low, kept, mixed)
            if last:
                out[p] = new.astype(BF)
                tail(p)
            else:
                acc_out[:, p * PAIR:(p + 1) * PAIR] = new
    if last:
        out[PAIRS] = stats.astype(BF)
        tail(PAIRS)
    else:
        stat_out[...] = stats


def attend(q, pieces, w_key, w_value, state):
    first = state is None
    rows = q.shape[0]
    count = sum(p.shape[0] for p in pieces)
    acc = jax.ShapeDtypeStruct((rows, PAIRS * PAIR), F32)
    stats = jax.ShapeDtypeStruct((rows, PAIR), F32)
    args = [q, *pieces, w_key, w_value] + ([] if first else list(state))
    wide = w_key.shape[0]
    return pl.pallas_call(
        functools.partial(attend_kernel, len(pieces), first, False),
        out_shape=(acc, stats),
        in_specs=[VMEM] * len(args),
        out_specs=(VMEM, VMEM),
        scratch_shapes=[
            pltpu.VMEM((PAIRS * PAIR, count), BF),
            pltpu.VMEM((PAIRS, count, 2 * PAIR), BF),
        ],
        cost_estimate=pl.CostEstimate(
            flops=16 * rows * count * wide + 4 * count * wide * wide,
            bytes_accessed=count * wide * 2 + rows * wide * 8,
            transcendentals=rows * count * HEADS,
        ),
        compiler_params=pltpu.CompilerParams(vmem_limit_bytes=56 * 1024 * 1024),
    )(*args)


def finish_kernel(outer, group, pieces, *refs):
    args = refs[:pieces + 5]
    w_out, mlp_gain, w_hidden, w_back, w_flow, valid, flow = refs[pieces + 5:pieces + 12]
    packed, got, keys, vals, send_sem, recv_sem = refs[pieces + 12:]
    ahead, across = peers(outer, group)
    greet([ahead(-k) for k in range(1, outer)])
    rows = got.shape[2]
    copies = []

    def tail(p):
        for k in range(1, outer):
            copy = pltpu.make_async_remote_copy(
                src_ref=packed.at[p, pl.ds(k * rows, rows)], dst_ref=got.at[p, k],
                send_sem=send_sem.at[p, k], recv_sem=recv_sem.at[p, k],
                device_id=ahead(-k), device_id_type=MESH,
            )
            copy.start()
            copies.append(copy)

    attend_kernel(pieces, False, True, *args, packed, keys, vals, tail=tail)
    for copy in copies:
        copy.wait()

    def part(k, p):
        return packed[p, :rows, :] if k == 0 else got[p, k]

    levels = []
    for k in range(outer):
        st = part(k, PAIRS).astype(F32)
        levels.append(
            st[:, :HEADS] + st[:, HEADS:2 * HEADS] + st[:, 2 * HEADS:3 * HEADS]
        )
    best = functools.reduce(jnp.maximum, levels)
    shares = [jnp.exp(level - best) for level in levels]
    total = functools.reduce(jnp.add, shares)
    shares = [s / total for s in shares]
    half = lax.broadcasted_iota(jnp.int32, (rows, PAIR), 1) < DH
    projected = jnp.zeros((rows, w_out.shape[1]), F32)
    for p in range(PAIRS):
        mixed = jnp.zeros((rows, PAIR), F32)
        for k, s in enumerate(shares):
            weight = jnp.where(half, s[:, 2 * p:2 * p + 1], s[:, 2 * p + 1:2 * p + 2])
            mixed = mixed + weight * part(k, p).astype(F32)
        projected = projected + jnp.dot(
            mixed.astype(BF), w_out[p * PAIR:(p + 1) * PAIR, :], preferred_element_type=F32
        )
    z = layer_norm(projected, mlp_gain[...])
    pre = jnp.dot(z.astype(BF), w_hidden[...], preferred_element_type=F32)
    hidden = (0.5 * pre * (1.0 + lax.erf(pre * (0.5 ** 0.5)))).astype(BF)
    u = (z + jnp.dot(hidden, w_back[...], preferred_element_type=F32)).astype(BF)
    res = lax.dot_general(
        w_flow[...], u, (((1,), (1,)), ((), ())), preferred_element_type=F32
    )
    flow[...] = res * valid[...].astype(F32)


def local(
    queries,
    tile_ids,
    tile_table,
    valid,
    latents,
    lat_gain,
    query_gain,
    w_query,
    w_key,
    w_value,
    w_out,
    mlp_gain,
    w_hidden,
    w_back,
    w_flow,
):
    pb, lat = lax.axis_size("pb"), lax.axis_size("lat")
    both = ("pb", "lat")
    outer = math.gcd(pb, lat)
    inner = pb // outer
    group = inner * lat
    devices = pb * lat
    rows, depth = queries.shape
    share = rows // lat
    own_rows, wide = latents.shape
    tiles = tile_table.shape[0]

    def swap(value, stride):
        pairs = [(i, i ^ stride) for i in range(devices)]
        return lax.ppermute(value, both, pairs)

    strides = [1 << i for i in range(1, group.bit_length() - 1)]
    assert 1 << (len(strides) + 1) == group
    half = own_rows // 2
    da = w_query.shape[1]
    q, held_a, held_b = pl.pallas_call(
        functools.partial(prepare_kernel, outer, group, strides[0], strides[-1]),
        out_shape=(
            jax.ShapeDtypeStruct((outer * share, da), BF),
            jax.ShapeDtypeStruct((own_rows, wide), BF),
            jax.ShapeDtypeStruct((own_rows, wide), BF),
        ),
        in_specs=[VMEM] * 7,
        out_specs=(VMEM,) * 3,
        scratch_shapes=[pltpu.VMEM((half, wide), BF)] * 4 + [
            pltpu.VMEM((share, da), BF),
            pltpu.VMEM((outer, share, da), BF),
            pltpu.SemaphoreType.DMA((outer + 2,)),
            pltpu.SemaphoreType.DMA((outer + 2,)),
        ],
        compiler_params=pltpu.CompilerParams(
            collective_id=0, has_side_effects=True, vmem_limit_bytes=32 * 1024 * 1024
        ),
    )(
        queries,
        tile_ids.reshape(lat, share),
        tile_table,
        latents,
        lat_gain.reshape(1, wide),
        query_gain.reshape(1, depth),
        w_query,
    )
    held = [held_a, held_b]
    orders = [strides, strides[::-1]]
    near = [swap(piece, 1) for piece in held]
    far = [swap(held[c], orders[c][1 % len(strides)]) for c in range(2)]
    state = attend(q, held, w_key, w_value, None)
    pending = near
    for j in range(1, len(strides)):
        far, state = lax.optimization_barrier((far, state))
        arrived = far
        near = [swap(piece, 1) for piece in arrived]
        if j + 1 < len(strides):
            held = [jnp.concatenate([held[c], arrived[c]]) for c in range(2)]
            far = [swap(held[c], orders[c][j + 1]) for c in range(2)]
        state = attend(q, pending, w_key, w_value, state)
        pending = arrived + near
    count = sum(p.shape[0] for p in pending)
    return pl.pallas_call(
        functools.partial(finish_kernel, outer, group, len(pending)),
        out_shape=jax.ShapeDtypeStruct((w_flow.shape[0], share), F32),
        in_specs=[VMEM] * (len(pending) + 11),
        out_specs=VMEM,
        scratch_shapes=[
            pltpu.VMEM((PAIRS + 1, outer * share, PAIR), BF),
            pltpu.VMEM((PAIRS + 1, outer, share, PAIR), BF),
            pltpu.VMEM((da, count), BF),
            pltpu.VMEM((PAIRS, count, 2 * PAIR), BF),
            pltpu.SemaphoreType.DMA((PAIRS + 1, outer)),
            pltpu.SemaphoreType.DMA((PAIRS + 1, outer)),
        ],
        compiler_params=pltpu.CompilerParams(
            collective_id=1, has_side_effects=True, vmem_limit_bytes=56 * 1024 * 1024
        ),
    )(
        q, *pending, w_key, w_value, *state,
        w_out, mlp_gain.reshape(1, depth), w_hidden, w_back, w_flow,
        valid.reshape(1, share),
    )


def solution(mesh):
    placed = (
        P("pb", None),
        P("pb"),
        P(),
        P(("pb", "lat")),
        P(("pb", "lat"), None),
        P(),
        P(),
        P(),
        P(),
        P(),
        P(),
        P(),
        P(),
        P(),
        P(),
    )
    return jax.shard_map(
        local, mesh=mesh, in_specs=placed, out_specs=P(None, ("pb", "lat")), check_vma=False
    )
```
